256 devices in a mesh: seq: 64 (over z, y, x_lo), head: 4 (over x_hi, core).
Axes of the slice: x: 4 (x_hi: 2, x_lo: 2; x = x_hi * 2 + x_lo), y: 4, z: 8, core: 2. Of those that a mesh axis runs over, the one named last changes fastest.
Arguments:
- queries: bfloat16 [8192, 8192], P(('seq', 'head')), may hold values from -20 to 20
- keys: bfloat16 [8192, 1024], P(('seq', 'head')), may hold values from -8 to 8
- values: bfloat16 [8192, 1024], P(('seq', 'head')), may hold values from -6 to 6
Outputs:
- attended: bfloat16 [8192, 8192], P(('seq', 'head'))
The draws below stay inside these ranges and needn't reach their ends.
All inputs are finite; a program needn't handle non-finite values.
Results may differ from the reference program's by a relative error of at most 0.0059.
Values may be sent and summed in bfloat16 or wider, within the bound.
A program may use at most 64 MiB of HBM per device.

```python
import jax
import jax.numpy as jnp
from jax import lax

Q_HEADS = 64
KV_HEADS = 8
HEAD_DIM = 128
SEQ_LEN = 8192
GROUP = 8


def draw_queries(key, part):
    key = jax.random.fold_in(key, 1)
    columns = Q_HEADS * HEAD_DIM
    result = jnp.clip(jax.random.normal(key, (SEQ_LEN, columns), jnp.float32), -6.0, 6.0)
    return result.astype(jnp.bfloat16)


def draw_keys(key, part):
    key = jax.random.fold_in(key, 2)
    columns = KV_HEADS * HEAD_DIM
    result = jnp.clip(jax.random.normal(key, (SEQ_LEN, columns), jnp.float32), -6.0, 6.0)
    return result.astype(jnp.bfloat16)


def shard_levels(stream_key, extent, cuts, smallest, largest):
    gain, own = 1.0, jax.random.fold_in(stream_key, 6)
    for dim, blocks in cuts:
        draws = jnp.exp(jax.random.uniform(jax.random.fold_in(own, dim), (blocks,), jnp.float32, smallest / len(cuts), largest / len(cuts)))
        gain = gain * jnp.repeat(draws, extent[dim] // blocks).reshape([-1 if axis == dim else 1 for axis in range(len(extent))])
    return gain


def scatter_about(own_key, dims, scale, most, shards=(), kind=jnp.bfloat16):
    values = scale * jax.random.normal(own_key, dims, jnp.float32)
    if shards:
        values = values * shard_levels(own_key, dims, shards, -0.22, 0.18)
    return jnp.clip(values, -most, most).astype(kind)


def setup_inputs(seed: int = 0) -> dict:
    key_list = jax.random.split(jax.random.key(seed), 4)
    return {
        "queries": draw_queries(jax.random.fold_in(key_list[3], 71), 0),
        "keys": draw_keys(jax.random.fold_in(key_list[3], 71), 0),
        "values": scatter_about(key_list[2], (SEQ_LEN, KV_HEADS * HEAD_DIM), 1.0, 6.0, ((0, 256),)),
    }


def reference(queries, keys, values):
    length = queries.shape[0]
    q_heads = queries.reshape(length, Q_HEADS, HEAD_DIM)
    k_heads = keys.reshape(length, KV_HEADS, HEAD_DIM)
    v_heads = values.reshape(length, KV_HEADS, HEAD_DIM)
    position = jnp.arange(length, dtype=jnp.int32)
    causal = position[:, None] >= position[None, :]
    factor = HEAD_DIM ** -0.5

    def one_head(head):
        group = (head // GROUP).astype(jnp.int32)
        query = lax.dynamic_index_in_dim(q_heads, head, 1, keepdims=False)
        key_rows = lax.dynamic_index_in_dim(k_heads, group, 1, keepdims=False)
        value_rows = lax.dynamic_index_in_dim(v_heads, group, 1, keepdims=False)
        score = jnp.dot(query, key_rows.T, preferred_element_type=jnp.float32) * factor
        score = jnp.where(causal, score, -jnp.inf)
        top = jnp.max(score, axis=1, keepdims=True)
        weight = jnp.exp(score - top)
        total = jnp.sum(weight, axis=1, keepdims=True)
        mixed = jnp.dot(weight.astype(jnp.bfloat16), value_rows, preferred_element_type=jnp.float32)
        return (mixed / total).astype(jnp.bfloat16)

    result = lax.map(one_head, jnp.arange(Q_HEADS, dtype=jnp.int32))
    return jnp.transpose(result, (1, 0, 2)).reshape(length, Q_HEADS * HEAD_DIM)
```

```python
import jax
import jax.numpy as jnp
import numpy as np
from jax import lax
from jax.experimental import pallas as pl
from jax.experimental.pallas import tpu as pltpu
from jax.sharding import PartitionSpec as P

MESH = pl.DeviceIdType.MESH
HEAD_DIM = 128
GROUP = 8
WIDE = GROUP * HEAD_DIM
BLOCK = 32
PEERS = 8
ROWS = PEERS * BLOCK
PLANE = 4 * ROWS
RING = 8
SCALE = np.float32(HEAD_DIM**-0.5 / np.log(2.0))
LOW = np.float32(-1e30)
TRANSPOSED = (((1,), (1,)), ((), ()))
PIECES = 4
PIECE = WIDE // PIECES


def kernel(
    queries, keys, values, out,
    qbuf, kv, obuf, tops, sums, acc, score_a, score_b,
    local_sem, q_send, q_recv, kv_send, kv_recv, y_send, y_recv,
    ring_send, ring_recv, twin_send, twin_recv, o_send, o_recv,
):
    seq, head = lax.axis_index("seq"), lax.axis_index("head")
    x_lo, y, z = seq % 2, (seq // 2) % 4, seq // 8
    x_hi, core = head // 2, head % 2
    fold = ((y + 1) // 2) % 2
    me = (y // 2) * 4 + x_hi * 2 + x_lo

    def at(z_, y_, x_hi_, x_lo_, core_):
        return ((z_ * 4 + y_) * 2 + x_lo_, x_hi_ * 2 + core_)

    def peer(step):
        other = (me + step) % PEERS
        row = jnp.where(other >= 4, 3 - fold, fold)
        return other, at(z, row, (other % 4) // 2, other % 2, core)

    up, down = at((z + 1) % RING, y, x_hi, x_lo, core), at((z + RING - 1) % RING, y, x_hi, x_lo, core)
    beside = at(z, y + 1 - 2 * (y % 2), x_hi, x_lo, core)
    twin = at(z, y, x_hi, x_lo, 1 - core)

    barrier = pltpu.get_barrier_semaphore()
    for step in range(1, PEERS):
        pl.semaphore_signal(barrier, inc=1, device_id=peer(step)[1], device_id_type=MESH)
    for device in (up, down, beside, twin):
        pl.semaphore_signal(barrier, inc=1, device_id=device, device_id_type=MESH)
    pl.semaphore_wait(barrier, PEERS + 3)

    def part(core_, fold_):
        return pl.multiple_of((core_ * 2 + fold_) * ROWS, ROWS)

    def lanes(index, width):
        return pl.ds(pl.multiple_of(index * width, width), width)

    def remote(src, dst, send, recv, device):
        return pltpu.make_async_remote_copy(
            src_ref=src, dst_ref=dst, send_sem=send, recv_sem=recv, device_id=device, device_id_type=MESH
        )

    mine = pl.ds(pl.multiple_of(part(core, fold) + me * BLOCK, BLOCK), BLOCK)

    def kv_copy(step, which):
        other, device = peer(step)
        src = (keys, values)[which]
        return remote(
            src.at[:, lanes(other, HEAD_DIM)], kv.at[z, which, mine],
            kv_send.at[which, step], kv_recv.at[which, step], device,
        )

    def q_copy(step):
        other, device = peer(step)
        return remote(queries.at[:, lanes(other, WIDE)], qbuf.at[me], q_send.at[step], q_recv.at[step], device)

    for step in range(1, PEERS):
        for which in range(2):
            kv_copy(step, which).start()
    own = (
        pltpu.make_async_copy(keys.at[:, lanes(me, HEAD_DIM)], kv.at[z, 0, mine], local_sem.at[0]),
        pltpu.make_async_copy(values.at[:, lanes(me, HEAD_DIM)], kv.at[z, 1, mine], local_sem.at[1]),
        pltpu.make_async_copy(queries.at[:, lanes(me, WIDE)], qbuf.at[me], local_sem.at[2]),
    )
    for copy in own:
        copy.start()
    for step in range(1, PEERS):
        q_copy(step).start()

    def sub_ref(plane, core_, sub):
        return kv.at[plane, :, pl.ds(part(core_, fold if sub == 0 else 1 - fold), ROWS)]

    def ring_copy(way, hop, sub):
        plane = (z + (RING - (hop - 1) if way == 0 else hop - 1)) % RING
        ref = sub_ref(plane, core, sub)
        return remote(
            ref, ref, ring_send.at[way, hop, sub], ring_recv.at[way, hop, sub], up if way == 0 else down
        )

    def twin_copy(plane, sub):
        ref = sub_ref(plane, core, sub)
        return remote(ref, ref, twin_send.at[plane, sub], twin_recv.at[plane, sub], twin)

    y_ref = sub_ref(z, core, 0)
    y_copy = remote(y_ref, y_ref, y_send, y_recv, beside)

    for copy in own[:2]:
        copy.wait()
    for step in range(1, PEERS):
        for which in range(2):
            kv_copy(step, which).wait_recv()
    y_copy.start()
    ring_copy(0, 1, 0).start()
    ring_copy(1, 1, 0).start()
    twin_copy(z, 0).start()
    y_copy.wait_recv()
    ring_copy(0, 1, 1).start()
    ring_copy(1, 1, 1).start()
    twin_copy(z, 1).start()

    def item_q(i):
        return qbuf[:, :, i * HEAD_DIM : (i + 1) * HEAD_DIM].reshape(ROWS, HEAD_DIM)

    def query_position():
        row = lax.broadcasted_iota(jnp.int32, (ROWS, PLANE), 0)
        return token_position(row, core, fold)

    def token_position(index, core_, fold_):
        slot, xx = index // (4 * BLOCK), (index // BLOCK) % 4
        line = jnp.where(slot == 1, 3 - fold_, fold_)
        return line * ROWS + ((xx % 2) * 4 + (xx // 2) * 2 + core_) * BLOCK + index % BLOCK

    def key_position():
        index = lax.broadcasted_iota(jnp.int32, (ROWS, PLANE), 1)
        return token_position(index % ROWS, index // (2 * ROWS), (index // ROWS) % 2)

    scores = (score_a, score_b)

    def multiply(plane, i):
        scores[i % 2][...] = lax.dot_general(
            item_q(i), kv[plane, 0], TRANSPOSED, preferred_element_type=jnp.float32
        )

    def soften(plane, i, first):
        score = scores[i % 2][...]
        if first:
            score = jnp.where(query_position() >= key_position(), score, LOW)
        top = jnp.broadcast_to(jnp.max(score, axis=1, keepdims=True), (ROWS, HEAD_DIM))
        if not first:
            before = tops[i]
            top = jnp.maximum(before, top)
            rescale = jnp.exp2((before - top) * SCALE)
        weight = jnp.exp2((score - jnp.tile(top, (1, PLANE // HEAD_DIM))) * SCALE)
        tops[i] = top
        mixed = jnp.dot(weight.astype(jnp.bfloat16), kv[plane, 1], preferred_element_type=jnp.float32)
        partial = weight[:, :HEAD_DIM]
        for column in range(1, PLANE // HEAD_DIM):
            partial = partial + weight[:, column * HEAD_DIM : (column + 1) * HEAD_DIM]
        if first:
            acc[i], sums[i] = mixed, partial
        else:
            acc[i], sums[i] = acc[i] * rescale + mixed, sums[i] * rescale + partial

    def o_copy(step, piece):
        other, device = peer(step)
        columns = pl.ds(pl.multiple_of(me * WIDE + piece * PIECE, PIECE), PIECE)
        return remote(
            obuf.at[other, :, pl.ds(piece * PIECE, PIECE)], out.at[:, columns],
            o_send.at[step, piece], o_recv.at[step, piece], device,
        )

    def finish(i):
        total = jnp.sum(sums[i], axis=1, keepdims=True)
        result = (acc[i] / total).astype(jnp.bfloat16)
        obuf[:, :, i * HEAD_DIM : (i + 1) * HEAD_DIM] = result.reshape(PEERS, BLOCK, HEAD_DIM)
        if (i + 1) % (GROUP // PIECES) == 0:
            for step in range(1, PEERS):
                o_copy(step, i // (GROUP // PIECES)).start()

    def sweep(plane, first=False, last=False):
        multiply(plane, 0)
        for i in range(GROUP):
            if i + 1 < GROUP:
                multiply(plane, i + 1)
            soften(plane, i, first)
            if last:
                finish(i)

    twin_copy(z, 0).wait_recv()
    twin_copy(z, 1).wait_recv()
    own[2].wait()
    for step in range(1, PEERS):
        q_copy(step).wait_recv()
    sweep(z, first=True)

    def far(way, hop):
        return (z + (RING - hop if way == 0 else hop)) % RING

    for hop in (1, 2, 3):
        for sub in range(2):
            for way in range(2):
                ring_copy(way, hop, sub).wait_recv()
                if hop < 3 or way == sub:
                    ring_copy(way, hop + 1, sub).start()
                twin_copy(far(way, hop), sub).start()
        for way in range(2):
            plane = far(way, hop)
            twin_copy(plane, 0).wait_recv()
            twin_copy(plane, 1).wait_recv()

        def one(way, carry):
            plane = (z + jnp.where(way == 0, RING - hop, hop)) % RING

            @pl.when(plane < z)
            def _():
                sweep(plane)

            return carry

        lax.fori_loop(0, 2, one, 0)

    opposite = (z + 4) % RING
    for sub in range(2):
        ring_copy(sub, 4, sub).wait_recv()
        twin_copy(opposite, sub).start()
    for sub in range(2):
        twin_copy(opposite, sub).wait_recv()

    @pl.when(opposite < z)
    def _():
        sweep(opposite, last=True)

    @pl.when(opposite > z)
    def _():
        for i in range(GROUP):
            finish(i)

    own_out = pltpu.make_async_copy(obuf.at[me], out.at[:, lanes(me, WIDE)], local_sem.at[3])
    own_out.start()

    for step in range(1, PEERS):
        for which in range(2):
            kv_copy(step, which).wait_send()
        q_copy(step).wait_send()
    y_copy.wait_send()
    for way in range(2):
        for hop in (1, 2, 3, 4):
            for sub in range(2):
                if hop < 4 or way == sub:
                    ring_copy(way, hop, sub).wait_send()
    for plane in range(RING):
        for sub in range(2):
            twin_copy(plane, sub).wait_send()
    for piece in range(PIECES):
        for step in range(1, PEERS):
            o_copy(step, piece).wait()
    own_out.wait()


def on_device(queries, keys, values):
    anywhere = pl.BlockSpec(memory_space=pl.ANY)
    return pl.pallas_call(
        kernel,
        out_shape=jax.ShapeDtypeStruct(queries.shape, jnp.bfloat16),
        in_specs=[anywhere] * 3,
        out_specs=anywhere,
        scratch_shapes=[
            pltpu.VMEM((PEERS, BLOCK, WIDE), jnp.bfloat16),
            pltpu.VMEM((RING, 2, PLANE, HEAD_DIM), jnp.bfloat16),
            pltpu.VMEM((PEERS, BLOCK, WIDE), jnp.bfloat16),
            pltpu.VMEM((GROUP, ROWS, HEAD_DIM), jnp.float32),
            pltpu.VMEM((GROUP, ROWS, HEAD_DIM), jnp.float32),
            pltpu.VMEM((GROUP, ROWS, HEAD_DIM), jnp.float32),
            pltpu.VMEM((ROWS, PLANE), jnp.float32),
            pltpu.VMEM((ROWS, PLANE), jnp.float32),
            pltpu.SemaphoreType.DMA((4,)),
            pltpu.SemaphoreType.DMA((PEERS,)),
            pltpu.SemaphoreType.DMA((PEERS,)),
            pltpu.SemaphoreType.DMA((2, PEERS)),
            pltpu.SemaphoreType.DMA((2, PEERS)),
            pltpu.SemaphoreType.DMA,
            pltpu.SemaphoreType.DMA,
            pltpu.SemaphoreType.DMA((2, 5, 2)),
            pltpu.SemaphoreType.DMA((2, 5, 2)),
            pltpu.SemaphoreType.DMA((RING, 2)),
            pltpu.SemaphoreType.DMA((RING, 2)),
            pltpu.SemaphoreType.DMA((PEERS, PIECES)),
            pltpu.SemaphoreType.DMA((PEERS, PIECES)),
        ],
        compiler_params=pltpu.CompilerParams(
            collective_id=0, has_side_effects=True, vmem_limit_bytes=48 * 2**20
        ),
    )(queries, keys, values)


def solution(mesh):
    spec = P(("seq", "head"), None)
    return jax.shard_map(on_device, mesh=mesh, in_specs=(spec,) * 3, out_specs=spec, check_vma=False)
```

```python
import jax
import jax.numpy as jnp
import numpy as np
from jax import lax
from jax.experimental import pallas as pl
from jax.experimental.pallas import tpu as pltpu
from jax.sharding import PartitionSpec as P

MESH = pl.DeviceIdType.MESH
HEAD_DIM = 128
GROUP = 8
WIDE = GROUP * HEAD_DIM
BLOCK = 32
PLANES = 8
SIDE = 4
ROWS = GROUP * BLOCK
KEYS = SIDE * SIDE * 2 * BLOCK
PHASES = ((0, 1), (1, 3), (3, 5), (5, 7), (7, 8))
SCALE = np.float32(HEAD_DIM**-0.5 / np.log(2.0))
LOW = np.float32(-1e30)
TRANSPOSED = (((1,), (1,)), ((), ()))
NEAR_FIRST = (1, 7, 2, 6, 3, 5, 4)


def kernel(
    queries, keys, values, out,
    qbuf, kv, obuf, tops, sums, acc, score_a, score_b,
    local_sem, q_send, q_recv, kv_send, kv_recv, one_send, one_recv, two_send, two_recv,
    twin_send, twin_recv, o_send, o_recv,
):
    seq, head = lax.axis_index("seq"), lax.axis_index("head")
    x_lo, y, z = seq % 2, (seq // 2) % 4, seq // 8
    x_hi, core = head // 2, head % 2
    x, place = x_hi * 2 + x_lo, x_lo * 2 + x_hi

    def at(x_, y_, z_, core_):
        return ((z_ * 4 + y_) * 2 + x_ % 2, (x_ // 2) * 2 + core_)

    def along_z(step):
        other = (z + step) % PLANES
        return other, at(x, y, other, core)

    def along_x(step):
        return at((x + step) % SIDE, y, z, core)

    def along_y(step):
        return at(x, (y + step) % SIDE, z, core)

    twin = at(x, y, z, 1 - core)

    barrier = pltpu.get_barrier_semaphore()
    greeted = [along_z(step)[1] for step in NEAR_FIRST]
    greeted += [along(step) for along in (along_x, along_y) for step in (1, 2, 3)] + [twin]
    for device in greeted:
        pl.semaphore_signal(barrier, inc=1, device_id=device, device_id_type=MESH)
    pl.semaphore_wait(barrier, len(greeted))

    def lanes(index, width):
        return pl.ds(pl.multiple_of(index * width, width), width)

    def remote(src, dst, send, recv, device):
        return pltpu.make_async_remote_copy(
            src_ref=src, dst_ref=dst, send_sem=send, recv_sem=recv, device_id=device, device_id_type=MESH
        )

    def kv_copy(step, which):
        other, device = along_z(step)
        return remote(
            (keys, values)[which].at[:, lanes(other, HEAD_DIM)], kv.at[z, which, core, y, place],
            kv_send.at[which, step], kv_recv.at[which, step], device,
        )

    def q_copy(step):
        other, device = along_z(step)
        return remote(queries.at[:, lanes(other, WIDE)], qbuf.at[z], q_send.at[step], q_recv.at[step], device)

    for step in NEAR_FIRST:
        for which in range(2):
            kv_copy(step, which).start()
    own = (
        pltpu.make_async_copy(keys.at[:, lanes(z, HEAD_DIM)], kv.at[z, 0, core, y, place], local_sem.at[0]),
        pltpu.make_async_copy(values.at[:, lanes(z, HEAD_DIM)], kv.at[z, 1, core, y, place], local_sem.at[1]),
        pltpu.make_async_copy(queries.at[:, lanes(z, WIDE)], qbuf.at[z], local_sem.at[2]),
    )
    for copy in own:
        copy.start()
    for step in NEAR_FIRST:
        q_copy(step).start()

    def planes(phase):
        start, stop = PHASES[phase]
        return pl.ds(start, stop - start)

    def one_copy(phase, which, step):
        ref = kv.at[planes(phase), which, core, y, place]
        device = (along_x, along_y)[which](step)
        return remote(ref, ref, one_send.at[phase, which, step], one_recv.at[phase, which, step], device)

    def two_copy(phase, which, step):
        ref = (kv.at[planes(phase), 0, core, y], kv.at[planes(phase), 1, core, :, place])[which]
        device = (along_y, along_x)[which](step)
        return remote(ref, ref, two_send.at[phase, which, step], two_recv.at[phase, which, step], device)

    def twin_copy(phase):
        ref = kv.at[planes(phase), :, core]
        return remote(ref, ref, twin_send.at[phase], twin_recv.at[phase], twin)

    six = [(which, step) for step in (1, 3, 2) for which in range(2)]

    def spread(phase):
        for which, step in six:
            one_copy(phase, which, step).wait_recv()
        for which, step in six:
            two_copy(phase, which, step).start()

    def pair(phase):
        for which, step in six:
            two_copy(phase, which, step).wait_recv()
        twin_copy(phase).start()

    def slice_of(plane):
        block = qbuf[plane]
        return jnp.concatenate([block[:, h * HEAD_DIM : (h + 1) * HEAD_DIM] for h in range(GROUP)], axis=0)

    def visible(plane, key_plane):
        row = lax.broadcasted_iota(jnp.int32, (ROWS, KEYS), 0)
        index = lax.broadcasted_iota(jnp.int32, (ROWS, KEYS), 1)
        query = (y * SIDE + place) * (2 * BLOCK) + core * BLOCK + row % BLOCK
        key = (index // BLOCK) % (SIDE * SIDE) * (2 * BLOCK) + index // (KEYS // 2) * BLOCK + index % BLOCK
        return query + (plane - key_plane) * KEYS >= key

    scores = (score_a, score_b)

    def multiply(item, n):
        plane, key_plane, _ = item
        scores[n % 2][...] = lax.dot_general(
            slice_of(plane), kv[key_plane, 0].reshape(KEYS, HEAD_DIM), TRANSPOSED,
            preferred_element_type=jnp.float32,
        )

    def soften(item, n):
        plane, key_plane, masked = item
        first = key_plane == 0
        score = scores[n % 2][...]
        if masked:
            score = jnp.where(visible(plane, key_plane), score, LOW)
        top = jnp.broadcast_to(jnp.max(score, axis=1, keepdims=True), (ROWS, HEAD_DIM))
        if not first:
            before = tops[plane]
            top = jnp.maximum(before, top)
            rescale = jnp.exp2((before - top) * SCALE)
        weight = jnp.exp2((score - jnp.tile(top, (1, KEYS // HEAD_DIM))) * SCALE)
        tops[plane] = top
        mixed = jnp.dot(
            weight.astype(jnp.bfloat16), kv[key_plane, 1].reshape(KEYS, HEAD_DIM),
            preferred_element_type=jnp.float32,
        )
        partial = weight[:, :HEAD_DIM]
        for column in range(1, KEYS // HEAD_DIM):
            partial = partial + weight[:, column * HEAD_DIM : (column + 1) * HEAD_DIM]
        if first:
            acc[plane], sums[plane] = mixed, partial
        else:
            acc[plane], sums[plane] = acc[plane] * rescale + mixed, sums[plane] * rescale + partial

    def sweep(items):
        multiply(items[0], 0)
        for n, item in enumerate(items):
            if n + 1 < len(items):
                multiply(items[n + 1], n + 1)
            soften(item, n)
            if isinstance(item[0], int) and item[0] == item[1]:
                finish(item[0])

    def o_copy(plane):
        return remote(
            obuf.at[plane], out.at[:, lanes(z, WIDE)], o_send.at[plane], o_recv.at[z], at(x, y, plane, core)
        )

    own_out = pltpu.make_async_copy(obuf.at[z], out.at[:, lanes(z, WIDE)], local_sem.at[3])

    def finish(plane):
        total = jnp.sum(sums[plane], axis=1, keepdims=True)
        result = (acc[plane] / total).astype(jnp.bfloat16)
        for h in range(GROUP):
            obuf[plane, :, h * HEAD_DIM : (h + 1) * HEAD_DIM] = result[h * BLOCK : (h + 1) * BLOCK]
        pl.when(plane != z)(lambda: o_copy(plane).start())
        pl.when(plane == z)(lambda: own_out.start())

    for copy in own[:2]:
        copy.wait()
    for step in NEAR_FIRST:
        for which in range(2):
            kv_copy(step, which).wait_recv()
    for phase in range(len(PHASES)):
        for which, step in six:
            one_copy(phase, which, step).start()
    def follow(phase):
        for which, step in six:
            two_copy(phase - 1, which, step).wait_send()
        spread(phase)

    def steps(*near):
        return [((z + step) % PLANES, 0, True) for step in near]

    def rest(phase):
        start, stop = PHASES[phase]
        return [
            (plane, key_plane, plane == key_plane)
            for plane in range(start, PLANES)
            for key_plane in range(start, min(plane + 1, stop))
        ]

    spread(0)
    follow(1)
    pair(0)
    follow(2)
    own[2].wait()
    for step in (1, 7, 2, 6):
        q_copy(step).wait_recv()
    twin_copy(0).wait_recv()
    sweep(steps(0, 1, 7, 2, 6))
    pair(1)
    follow(3)
    for step in (3, 5, 4):
        q_copy(step).wait_recv()
    sweep(steps(3, 5, 4))
    finish(0)
    twin_copy(1).wait_recv()
    items = rest(1)
    sweep(items[:7])
    pair(2)
    follow(4)
    sweep(items[7:])
    pair(3)
    twin_copy(2).wait_recv()
    sweep(rest(2))
    pair(4)
    twin_copy(3).wait_recv()
    sweep(rest(3))
    twin_copy(4).wait_recv()
    sweep(rest(4))

    for which, step in six:
        two_copy(4, which, step).wait_send()
    for step in NEAR_FIRST:
        for which in range(2):
            kv_copy(step, which).wait_send()
        q_copy(step).wait_send()
    for phase in range(len(PHASES)):
        for which, step in six:
            one_copy(phase, which, step).wait_send()
        twin_copy(phase).wait_send()
    own_out.wait()
    for plane in range(PLANES):

        @pl.when(plane != z)
        def _():
            o_copy(plane).wait_send()
            ref = out.at[:, lanes(plane, WIDE)]
            remote(ref, ref, o_send.at[plane], o_recv.at[plane], at(x, y, plane, core)).wait_recv()


def on_device(queries, keys, values):
    anywhere = pl.BlockSpec(memory_space=pl.ANY)
    return pl.pallas_call(
        kernel,
        out_shape=jax.ShapeDtypeStruct(queries.shape, jnp.bfloat16),
        in_specs=[anywhere] * 3,
        out_specs=anywhere,
        scratch_shapes=[
            pltpu.VMEM((PLANES, BLOCK, WIDE), jnp.bfloat16),
            pltpu.VMEM((PLANES, 2, 2, SIDE, SIDE, BLOCK, HEAD_DIM), jnp.bfloat16),
            pltpu.VMEM((PLANES, BLOCK, WIDE), jnp.bfloat16),
            pltpu.VMEM((PLANES, ROWS, HEAD_DIM), jnp.float32),
            pltpu.VMEM((PLANES, ROWS, HEAD_DIM), jnp.float32),
            pltpu.VMEM((PLANES, ROWS, HEAD_DIM), jnp.float32),
            pltpu.VMEM((ROWS, KEYS), jnp.float32),
            pltpu.VMEM((ROWS, KEYS), jnp.float32),
            pltpu.SemaphoreType.DMA((4,)),
            pltpu.SemaphoreType.DMA((PLANES,)),
            pltpu.SemaphoreType.DMA((PLANES,)),
            pltpu.SemaphoreType.DMA((2, PLANES)),
            pltpu.SemaphoreType.DMA((2, PLANES)),
            pltpu.SemaphoreType.DMA((len(PHASES), 2, SIDE)),
            pltpu.SemaphoreType.DMA((len(PHASES), 2, SIDE)),
            pltpu.SemaphoreType.DMA((len(PHASES), 2, SIDE)),
            pltpu.SemaphoreType.DMA((len(PHASES), 2, SIDE)),
            pltpu.SemaphoreType.DMA((len(PHASES),)),
            pltpu.SemaphoreType.DMA((len(PHASES),)),
            pltpu.SemaphoreType.DMA((PLANES,)),
            pltpu.SemaphoreType.DMA((PLANES,)),
        ],
        compiler_params=pltpu.CompilerParams(
            collective_id=0, has_side_effects=True, vmem_limit_bytes=60 * 2**20
        ),
    )(queries, keys, values)


def solution(mesh):
    spec = P(("seq", "head"), None)
    return jax.shard_map(on_device, mesh=mesh, in_specs=(spec,) * 3, out_specs=spec, check_vma=False)
```

```python
import jax
import jax.numpy as jnp
import numpy as np
from jax import lax
from jax.experimental import pallas as pl
from jax.experimental.pallas import tpu as pltpu
from jax.sharding import PartitionSpec as P

MESH = pl.DeviceIdType.MESH
HEAD_DIM = 128
GROUP = 8
WIDE = GROUP * HEAD_DIM
BLOCK = 32
PLANES = 8
SIDE = 4
ROWS = GROUP * BLOCK
KEYS = SIDE * SIDE * 2 * BLOCK
PHASES = ((0, 1), (1, 3), (3, 5), (5, 7), (7, 8))
SCALE = np.float32(HEAD_DIM**-0.5 / np.log(2.0))
LOW = np.float32(-1e30)
TRANSPOSED = (((1,), (1,)), ((), ()))
NEAR_FIRST = (1, 7, 2, 6, 3, 5, 4)


def kernel(
    queries, keys, values, out,
    qbuf, kv, obuf, tops, sums, acc, score_a, score_b,
    local_sem, q_send, q_recv, kv_send, kv_recv, one_send, one_recv, two_send, two_recv,
    twin_send, twin_recv, o_send, o_recv,
):
    seq, head = lax.axis_index("seq"), lax.axis_index("head")
    x_lo, y, z = seq % 2, (seq // 2) % 4, seq // 8
    x_hi, core = head // 2, head % 2
    x, place = x_hi * 2 + x_lo, x_lo * 2 + x_hi

    def at(x_, y_, z_, core_):
        return ((z_ * 4 + y_) * 2 + x_ % 2, (x_ // 2) * 2 + core_)

    def along_z(step):
        other = (z + step) % PLANES
        return other, at(x, y, other, core)

    def along_x(step):
        return at((x + step) % SIDE, y, z, core)

    def along_y(step):
        return at(x, (y + step) % SIDE, z, core)

    twin = at(x, y, z, 1 - core)

    barrier = pltpu.get_barrier_semaphore()
    greeted = [along_z(step)[1] for step in NEAR_FIRST]
    greeted += [along(step) for along in (along_x, along_y) for step in (1, 2, 3)] + [twin]
    for device in greeted:
        pl.semaphore_signal(barrier, inc=1, device_id=device, device_id_type=MESH)
    pl.semaphore_wait(barrier, len(greeted))

    def lanes(index, width):
        return pl.ds(pl.multiple_of(index * width, width), width)

    def remote(src, dst, send, recv, device):
        return pltpu.make_async_remote_copy(
            src_ref=src, dst_ref=dst, send_sem=send, recv_sem=recv, device_id=device, device_id_type=MESH
        )

    def kv_copy(step, which):
        other, device = along_z(step)
        return remote(
            (keys, values)[which].at[:, lanes(other, HEAD_DIM)], kv.at[z, which, core, y, place],
            kv_send.at[which, step], kv_recv.at[which, step], device,
        )

    def q_copy(step):
        other, device = along_z(step)
        return remote(queries.at[:, lanes(other, WIDE)], qbuf.at[z], q_send.at[step], q_recv.at[step], device)

    for step in NEAR_FIRST:
        for which in range(2):
            kv_copy(step, which).start()
    own = (
        pltpu.make_async_copy(keys.at[:, lanes(z, HEAD_DIM)], kv.at[z, 0, core, y, place], local_sem.at[0]),
        pltpu.make_async_copy(values.at[:, lanes(z, HEAD_DIM)], kv.at[z, 1, core, y, place], local_sem.at[1]),
        pltpu.make_async_copy(queries.at[:, lanes(z, WIDE)], qbuf.at[z], local_sem.at[2]),
    )
    for copy in own:
        copy.start()
    for step in NEAR_FIRST:
        q_copy(step).start()

    def planes(phase):
        start, stop = PHASES[phase]
        return pl.ds(start, stop - start)

    def one_copy(phase, which, step):
        ref = kv.at[planes(phase), which, core, y, place]
        device = (along_x, along_y)[which](step)
        return remote(ref, ref, one_send.at[phase, which, step], one_recv.at[phase, which, step], device)

    def two_copy(phase, which, step):
        ref = (kv.at[planes(phase), 0, core, y], kv.at[planes(phase), 1, core, :, place])[which]
        device = (along_y, along_x)[which](step)
        return remote(ref, ref, two_send.at[phase, which, step], two_recv.at[phase, which, step], device)

    def twin_copy(phase):
        ref = kv.at[planes(phase), :, core]
        return remote(ref, ref, twin_send.at[phase], twin_recv.at[phase], twin)

    six = [(which, step) for step in (1, 3, 2) for which in range(2)]

    def spread(phase):
        for which, step in six:
            one_copy(phase, which, step).wait_recv()
        for which, step in six:
            two_copy(phase, which, step).start()

    def pair(phase):
        for which, step in six:
            two_copy(phase, which, step).wait_recv()
        twin_copy(phase).start()

    def slice_of(plane):
        block = qbuf[plane]
        return jnp.concatenate([block[:, h * HEAD_DIM : (h + 1) * HEAD_DIM] for h in range(GROUP)], axis=0)

    def visible(plane, key_plane):
        row = lax.broadcasted_iota(jnp.int32, (ROWS, KEYS), 0)
        index = lax.broadcasted_iota(jnp.int32, (ROWS, KEYS), 1)
        query = (y * SIDE + place) * (2 * BLOCK) + core * BLOCK + row % BLOCK
        key = (index // BLOCK) % (SIDE * SIDE) * (2 * BLOCK) + index // (KEYS // 2) * BLOCK + index % BLOCK
        return query + (plane - key_plane) * KEYS >= key

    scores = (score_a, score_b)

    def multiply(item, n):
        plane, key_plane, _ = item
        scores[n % 2][...] = lax.dot_general(
            slice_of(plane), kv[key_plane, 0].reshape(KEYS, HEAD_DIM), TRANSPOSED,
            preferred_element_type=jnp.float32,
        )

    def soften(item, n):
        plane, key_plane, masked = item
        first = key_plane == 0
        score = scores[n % 2][...]
        if masked:
            score = jnp.where(visible(plane, key_plane), score, LOW)
        top = jnp.broadcast_to(jnp.max(score, axis=1, keepdims=True), (ROWS, HEAD_DIM))
        if not first:
            before = tops[plane]
            top = jnp.maximum(before, top)
            rescale = jnp.exp2((before - top) * SCALE)
        weight = jnp.exp2((score - jnp.tile(top, (1, KEYS // HEAD_DIM))) * SCALE)
        tops[plane] = top
        mixed = jnp.dot(
            weight.astype(jnp.bfloat16), kv[key_plane, 1].reshape(KEYS, HEAD_DIM),
            preferred_element_type=jnp.float32,
        )
        partial = weight[:, :HEAD_DIM]
        for column in range(1, KEYS // HEAD_DIM):
            partial = partial + weight[:, column * HEAD_DIM : (column + 1) * HEAD_DIM]
        if first:
            acc[plane], sums[plane] = mixed, partial
        else:
            acc[plane], sums[plane] = acc[plane] * rescale + mixed, sums[plane] * rescale + partial

    def sweep(items):
        multiply(items[0], 0)
        for n, item in enumerate(items):
            if n + 1 < len(items):
                multiply(items[n + 1], n + 1)
            soften(item, n)
            if isinstance(item[0], int) and item[0] == item[1]:
                finish(item[0])

    def o_copy(plane):
        return remote(
            obuf.at[plane], out.at[:, lanes(z, WIDE)], o_send.at[plane], o_recv.at[z], at(x, y, plane, core)
        )

    own_out = pltpu.make_async_copy(obuf.at[z], out.at[:, lanes(z, WIDE)], local_sem.at[3])

    def finish(plane):
        total = jnp.sum(sums[plane], axis=1, keepdims=True)
        result = (acc[plane] / total).astype(jnp.bfloat16)
        for h in range(GROUP):
            obuf[plane, :, h * HEAD_DIM : (h + 1) * HEAD_DIM] = result[h * BLOCK : (h + 1) * BLOCK]
        pl.when(plane != z)(lambda: o_copy(plane).start())
        pl.when(plane == z)(lambda: own_out.start())

    for copy in own[:2]:
        copy.wait()
    for step in NEAR_FIRST:
        for which in range(2):
            kv_copy(step, which).wait_recv()
    for phase in range(len(PHASES)):
        for which, step in six:
            one_copy(phase, which, step).start()
    def follow(phase):
        for which, step in six:
            two_copy(phase - 1, which, step).wait_send()
        spread(phase)

    def steps(*near):
        return [((z + step) % PLANES, 0, True) for step in near]

    def pairs(plane, start, stop):
        return [(plane, key_plane, plane == key_plane) for key_plane in range(start, stop)]

    spread(0)
    follow(1)
    pair(0)
    follow(2)
    own[2].wait()
    for step in (1, 7, 2, 6):
        q_copy(step).wait_recv()
    twin_copy(0).wait_recv()
    sweep(steps(0, 1, 7, 2, 6))
    pair(1)
    follow(3)
    for step in (3, 5, 4):
        q_copy(step).wait_recv()
    sweep(steps(3, 5, 4))
    finish(0)
    twin_copy(1).wait_recv()
    sweep(pairs(1, 1, 2) + pairs(2, 1, 3) + pairs(3, 1, 3))
    pair(2)
    follow(4)
    sweep(pairs(4, 1, 3) + pairs(5, 1, 3))
    twin_copy(2).wait_recv()
    sweep(pairs(3, 3, 4) + pairs(4, 3, 5) + pairs(5, 3, 4))
    pair(3)
    sweep(pairs(5, 4, 5) + pairs(6, 1, 3))
    twin_copy(3).wait_recv()
    sweep(pairs(5, 5, 6) + pairs(6, 3, 7))
    pair(4)
    sweep(pairs(7, 1, 7))
    twin_copy(4).wait_recv()
    sweep(pairs(7, 7, 8))

    for which, step in six:
        two_copy(4, which, step).wait_send()
    for step in NEAR_FIRST:
        for which in range(2):
            kv_copy(step, which).wait_send()
        q_copy(step).wait_send()
    for phase in range(len(PHASES)):
        for which, step in six:
            one_copy(phase, which, step).wait_send()
        twin_copy(phase).wait_send()
    own_out.wait()
    for plane in range(PLANES):

        @pl.when(plane != z)
        def _():
            o_copy(plane).wait_send()
            ref = out.at[:, lanes(plane, WIDE)]
            remote(ref, ref, o_send.at[plane], o_recv.at[plane], at(x, y, plane, core)).wait_recv()


def on_device(queries, keys, values):
    anywhere = pl.BlockSpec(memory_space=pl.ANY)
    return pl.pallas_call(
        kernel,
        out_shape=jax.ShapeDtypeStruct(queries.shape, jnp.bfloat16),
        in_specs=[anywhere] * 3,
        out_specs=anywhere,
        scratch_shapes=[
            pltpu.VMEM((PLANES, BLOCK, WIDE), jnp.bfloat16),
            pltpu.VMEM((PLANES, 2, 2, SIDE, SIDE, BLOCK, HEAD_DIM), jnp.bfloat16),
            pltpu.VMEM((PLANES, BLOCK, WIDE), jnp.bfloat16),
            pltpu.VMEM((PLANES, ROWS, HEAD_DIM), jnp.float32),
            pltpu.VMEM((PLANES, ROWS, HEAD_DIM), jnp.float32),
            pltpu.VMEM((PLANES, ROWS, HEAD_DIM), jnp.float32),
            pltpu.VMEM((ROWS, KEYS), jnp.float32),
            pltpu.VMEM((ROWS, KEYS), jnp.float32),
            pltpu.SemaphoreType.DMA((4,)),
            pltpu.SemaphoreType.DMA((PLANES,)),
            pltpu.SemaphoreType.DMA((PLANES,)),
            pltpu.SemaphoreType.DMA((2, PLANES)),
            pltpu.SemaphoreType.DMA((2, PLANES)),
            pltpu.SemaphoreType.DMA((len(PHASES), 2, SIDE)),
            pltpu.SemaphoreType.DMA((len(PHASES), 2, SIDE)),
            pltpu.SemaphoreType.DMA((len(PHASES), 2, SIDE)),
            pltpu.SemaphoreType.DMA((len(PHASES), 2, SIDE)),
            pltpu.SemaphoreType.DMA((len(PHASES),)),
            pltpu.SemaphoreType.DMA((len(PHASES),)),
            pltpu.SemaphoreType.DMA((PLANES,)),
            pltpu.SemaphoreType.DMA((PLANES,)),
        ],
        compiler_params=pltpu.CompilerParams(
            collective_id=0, has_side_effects=True, vmem_limit_bytes=60 * 2**20
        ),
    )(queries, keys, values)


def solution(mesh):
    spec = P(("seq", "head"), None)
    return jax.shard_map(on_device, mesh=mesh, in_specs=(spec,) * 3, out_specs=spec, check_vma=False)
```

```python
import jax
import jax.numpy as jnp
import numpy as np
from jax import lax
from jax.experimental import pallas as pl
from jax.experimental.pallas import tpu as pltpu
from jax.sharding import PartitionSpec as P

MESH = pl.DeviceIdType.MESH
HEAD_DIM = 128
GROUP = 8
WIDE = GROUP * HEAD_DIM
BLOCK = 32
PLANES = 8
SIDE = 4
ROWS = GROUP * BLOCK
KEYS = SIDE * SIDE * 2 * BLOCK
PHASES = ((0, 1), (1, 3), (3, 5), (5, 7), (7, 8))
SCALE = np.float32(HEAD_DIM**-0.5 / np.log(2.0))
LOW = np.float32(-1e30)
TRANSPOSED = (((1,), (1,)), ((), ()))
NEAR_FIRST = (1, 7, 2, 6, 3, 5, 4)


def kernel(
    queries, keys, values, out,
    qbuf, kv, obuf, tops, sums, acc, score_a, score_b,
    local_sem, q_send, q_recv, kv_send, kv_recv, one_send, one_recv, two_send, two_recv,
    twin_send, twin_recv, o_send, o_recv,
):
    seq, head = lax.axis_index("seq"), lax.axis_index("head")
    x_lo, y, z = seq % 2, (seq // 2) % 4, seq // 8
    x_hi, core = head // 2, head % 2
    x, place = x_hi * 2 + x_lo, x_lo * 2 + x_hi

    def at(x_, y_, z_, core_):
        return ((z_ * 4 + y_) * 2 + x_ % 2, (x_ // 2) * 2 + core_)

    def along_z(step):
        other = (z + step) % PLANES
        return other, at(x, y, other, core)

    def along_x(step):
        return at((x + step) % SIDE, y, z, core)

    def along_y(step):
        return at(x, (y + step) % SIDE, z, core)

    twin = at(x, y, z, 1 - core)

    barrier = pltpu.get_barrier_semaphore()
    greeted = [along_z(step)[1] for step in NEAR_FIRST]
    greeted += [along(step) for along in (along_x, along_y) for step in (1, 2, 3)] + [twin]
    for device in greeted:
        pl.semaphore_signal(barrier, inc=1, device_id=device, device_id_type=MESH)
    pl.semaphore_wait(barrier, len(greeted))

    def lanes(index, width):
        return pl.ds(pl.multiple_of(index * width, width), width)

    def remote(src, dst, send, recv, device):
        return pltpu.make_async_remote_copy(
            src_ref=src, dst_ref=dst, send_sem=send, recv_sem=recv, device_id=device, device_id_type=MESH
        )

    def kv_copy(step, which):
        other, device = along_z(step)
        return remote(
            (keys, values)[which].at[:, lanes(other, HEAD_DIM)], kv.at[z, which, core, y, place],
            kv_send.at[which, step], kv_recv.at[which, step], device,
        )

    def q_copy(step):
        other, device = along_z(step)
        return remote(queries.at[:, lanes(other, WIDE)], qbuf.at[z], q_send.at[step], q_recv.at[step], device)

    for step in NEAR_FIRST:
        for which in range(2):
            kv_copy(step, which).start()
    own = (
        pltpu.make_async_copy(keys.at[:, lanes(z, HEAD_DIM)], kv.at[z, 0, core, y, place], local_sem.at[0]),
        pltpu.make_async_copy(values.at[:, lanes(z, HEAD_DIM)], kv.at[z, 1, core, y, place], local_sem.at[1]),
        pltpu.make_async_copy(queries.at[:, lanes(z, WIDE)], qbuf.at[z], local_sem.at[2]),
    )
    for copy in own:
        copy.start()
    for step in NEAR_FIRST:
        q_copy(step).start()

    def planes(phase):
        start, stop = PHASES[phase]
        return pl.ds(start, stop - start)

    def one_copy(part, which, step):
        some = planes(0) if part == 0 else pl.ds(PHASES[1][0], PLANES - PHASES[1][0])
        ref = kv.at[some, which, core, y, place]
        device = (along_x, along_y)[which](step)
        return remote(ref, ref, one_send.at[part, which, step], one_recv.at[part, which, step], device)

    def two_copy(phase, which, step):
        ref = (kv.at[planes(phase), 0, core, y], kv.at[planes(phase), 1, core, :, place])[which]
        device = (along_y, along_x)[which](step)
        return remote(ref, ref, two_send.at[phase, which, step], two_recv.at[phase, which, step], device)

    def twin_copy(phase):
        ref = kv.at[planes(phase), :, core]
        return remote(ref, ref, twin_send.at[phase], twin_recv.at[phase], twin)

    six = [(which, step) for step in (1, 3, 2) for which in range(2)]

    def spread(phase):
        if phase < 2:
            for which, step in six:
                one_copy(phase, which, step).wait_recv()
        for which, step in six:
            two_copy(phase, which, step).start()

    def pair(phase):
        for which, step in six:
            two_copy(phase, which, step).wait_recv()
        twin_copy(phase).start()

    def slice_of(plane):
        block = qbuf[plane]
        return jnp.concatenate([block[:, h * HEAD_DIM : (h + 1) * HEAD_DIM] for h in range(GROUP)], axis=0)

    def visible(plane, key_plane):
        row = lax.broadcasted_iota(jnp.int32, (ROWS, KEYS), 0)
        index = lax.broadcasted_iota(jnp.int32, (ROWS, KEYS), 1)
        query = (y * SIDE + place) * (2 * BLOCK) + core * BLOCK + row % BLOCK
        key = (index // BLOCK) % (SIDE * SIDE) * (2 * BLOCK) + index // (KEYS // 2) * BLOCK + index % BLOCK
        return query + (plane - key_plane) * KEYS >= key

    scores = (score_a, score_b)

    def multiply(item, n):
        plane, key_plane, _ = item
        scores[n % 2][...] = lax.dot_general(
            slice_of(plane), kv[key_plane, 0].reshape(KEYS, HEAD_DIM), TRANSPOSED,
            preferred_element_type=jnp.float32,
        )

    def soften(item, n):
        plane, key_plane, masked = item
        first = key_plane == 0
        score = scores[n % 2][...]
        if masked:
            score = jnp.where(visible(plane, key_plane), score, LOW)
        top = jnp.broadcast_to(jnp.max(score, axis=1, keepdims=True), (ROWS, HEAD_DIM))
        if not first:
            before = tops[plane]
            top = jnp.maximum(before, top)
            rescale = jnp.exp2((before - top) * SCALE)
        weight = jnp.exp2((score - jnp.tile(top, (1, KEYS // HEAD_DIM))) * SCALE)
        tops[plane] = top
        mixed = jnp.dot(
            weight.astype(jnp.bfloat16), kv[key_plane, 1].reshape(KEYS, HEAD_DIM),
            preferred_element_type=jnp.float32,
        )
        partial = weight[:, :HEAD_DIM]
        for column in range(1, KEYS // HEAD_DIM):
            partial = partial + weight[:, column * HEAD_DIM : (column + 1) * HEAD_DIM]
        if first:
            acc[plane], sums[plane] = mixed, partial
        else:
            acc[plane], sums[plane] = acc[plane] * rescale + mixed, sums[plane] * rescale + partial

    def sweep(items):
        multiply(items[0], 0)
        for n, item in enumerate(items):
            if n + 1 < len(items):
                multiply(items[n + 1], n + 1)
            soften(item, n)
            if isinstance(item[0], int) and item[0] == item[1]:
                finish(item[0])

    def o_copy(plane):
        return remote(
            obuf.at[plane], out.at[:, lanes(z, WIDE)], o_send.at[plane], o_recv.at[z], at(x, y, plane, core)
        )

    own_out = pltpu.make_async_copy(obuf.at[z], out.at[:, lanes(z, WIDE)], local_sem.at[3])

    def finish(plane):
        total = jnp.sum(sums[plane], axis=1, keepdims=True)
        result = (acc[plane] / total).astype(jnp.bfloat16)
        for h in range(GROUP):
            obuf[plane, :, h * HEAD_DIM : (h + 1) * HEAD_DIM] = result[h * BLOCK : (h + 1) * BLOCK]
        pl.when(plane != z)(lambda: o_copy(plane).start())
        pl.when(plane == z)(lambda: own_out.start())

    for copy in own[:2]:
        copy.wait()
    for step in NEAR_FIRST:
        for which in range(2):
            kv_copy(step, which).wait_recv()
    for part in range(2):
        for which, step in six:
            one_copy(part, which, step).start()
    def follow(phase):
        for which, step in six:
            two_copy(phase - 1, which, step).wait_send()
        spread(phase)

    def steps(*near):
        return [((z + step) % PLANES, 0, True) for step in near]

    def pairs(plane, start, stop):
        return [(plane, key_plane, plane == key_plane) for key_plane in range(start, stop)]

    spread(0)
    follow(1)
    pair(0)
    follow(2)
    own[2].wait()
    for step in (1, 7, 2, 6):
        q_copy(step).wait_recv()
    twin_copy(0).wait_recv()
    sweep(steps(0, 1, 7, 2, 6))
    pair(1)
    follow(3)
    for step in (3, 5, 4):
        q_copy(step).wait_recv()
    sweep(steps(3, 5, 4))
    finish(0)
    twin_copy(1).wait_recv()
    sweep(pairs(1, 1, 2) + pairs(2, 1, 3) + pairs(3, 1, 3))
    pair(2)
    follow(4)
    sweep(pairs(4, 1, 3) + pairs(5, 1, 3))
    twin_copy(2).wait_recv()
    sweep(pairs(3, 3, 4) + pairs(4, 3, 5) + pairs(5, 3, 4))
    pair(3)
    sweep(pairs(5, 4, 5) + pairs(6, 1, 3))
    twin_copy(3).wait_recv()
    sweep(pairs(5, 5, 6) + pairs(6, 3, 7))
    pair(4)
    sweep(pairs(7, 1, 7))
    twin_copy(4).wait_recv()
    sweep(pairs(7, 7, 8))

    for which, step in six:
        two_copy(4, which, step).wait_send()
    for step in NEAR_FIRST:
        for which in range(2):
            kv_copy(step, which).wait_send()
        q_copy(step).wait_send()
    for part in range(2):
        for which, step in six:
            one_copy(part, which, step).wait_send()
    for phase in range(len(PHASES)):
        twin_copy(phase).wait_send()
    own_out.wait()
    for plane in range(PLANES):

        @pl.when(plane != z)
        def _():
            o_copy(plane).wait_send()
            ref = out.at[:, lanes(plane, WIDE)]
            remote(ref, ref, o_send.at[plane], o_recv.at[plane], at(x, y, plane, core)).wait_recv()


def on_device(queries, keys, values):
    anywhere = pl.BlockSpec(memory_space=pl.ANY)
    return pl.pallas_call(
        kernel,
        out_shape=jax.ShapeDtypeStruct(queries.shape, jnp.bfloat16),
        in_specs=[anywhere] * 3,
        out_specs=anywhere,
        scratch_shapes=[
            pltpu.VMEM((PLANES, BLOCK, WIDE), jnp.bfloat16),
            pltpu.VMEM((PLANES, 2, 2, SIDE, SIDE, BLOCK, HEAD_DIM), jnp.bfloat16),
            pltpu.VMEM((PLANES, BLOCK, WIDE), jnp.bfloat16),
            pltpu.VMEM((PLANES, ROWS, HEAD_DIM), jnp.float32),
            pltpu.VMEM((PLANES, ROWS, HEAD_DIM), jnp.float32),
            pltpu.VMEM((PLANES, ROWS, HEAD_DIM), jnp.float32),
            pltpu.VMEM((ROWS, KEYS), jnp.float32),
            pltpu.VMEM((ROWS, KEYS), jnp.float32),
            pltpu.SemaphoreType.DMA((4,)),
            pltpu.SemaphoreType.DMA((PLANES,)),
            pltpu.SemaphoreType.DMA((PLANES,)),
            pltpu.SemaphoreType.DMA((2, PLANES)),
            pltpu.SemaphoreType.DMA((2, PLANES)),
            pltpu.SemaphoreType.DMA((2, 2, SIDE)),
            pltpu.SemaphoreType.DMA((2, 2, SIDE)),
            pltpu.SemaphoreType.DMA((len(PHASES), 2, SIDE)),
            pltpu.SemaphoreType.DMA((len(PHASES), 2, SIDE)),
            pltpu.SemaphoreType.DMA((len(PHASES),)),
            pltpu.SemaphoreType.DMA((len(PHASES),)),
            pltpu.SemaphoreType.DMA((PLANES,)),
            pltpu.SemaphoreType.DMA((PLANES,)),
        ],
        compiler_params=pltpu.CompilerParams(
            collective_id=0, has_side_effects=True, vmem_limit_bytes=60 * 2**20
        ),
    )(queries, keys, values)


def solution(mesh):
    spec = P(("seq", "head"), None)
    return jax.shard_map(on_device, mesh=mesh, in_specs=(spec,) * 3, out_specs=spec, check_vma=False)
```

```python
import jax
import jax.numpy as jnp
import numpy as np
from jax import lax
from jax.experimental import pallas as pl
from jax.experimental.pallas import tpu as pltpu
from jax.sharding import PartitionSpec as P

MESH = pl.DeviceIdType.MESH
HEAD_DIM = 128
GROUP = 8
WIDE = GROUP * HEAD_DIM
BLOCK = 32
PLANES = 8
SIDE = 4
ROWS = GROUP * BLOCK
KEYS = SIDE * SIDE * 2 * BLOCK
PHASES = ((0, 1), (1, 3), (3, 5), (5, 7), (7, 8))
SCALE = np.float32(HEAD_DIM**-0.5 / np.log(2.0))
LOW = np.float32(-1e30)
TRANSPOSED = (((1,), (1,)), ((), ()))
NEAR_FIRST = (1, 7, 2, 6, 3, 5, 4)


def kernel(
    queries, keys, values, out,
    qbuf, kv, obuf, tops, sums, acc, score_a, score_b,
    local_sem, q_send, q_recv, kv_send, kv_recv, one_send, one_recv, two_send, two_recv,
    twin_send, twin_recv, o_send, o_recv,
):
    seq, head = lax.axis_index("seq"), lax.axis_index("head")
    x_lo, y, z = seq % 2, (seq // 2) % 4, seq // 8
    x_hi, core = head // 2, head % 2
    x, place = x_hi * 2 + x_lo, x_lo * 2 + x_hi

    def at(x_, y_, z_, core_):
        return ((z_ * 4 + y_) * 2 + x_ % 2, (x_ // 2) * 2 + core_)

    def along_z(step):
        other = (z + step) % PLANES
        return other, at(x, y, other, core)

    def along_x(step):
        return at((x + step) % SIDE, y, z, core)

    def along_y(step):
        return at(x, (y + step) % SIDE, z, core)

    twin = at(x, y, z, 1 - core)

    def lanes(index, width):
        return pl.ds(pl.multiple_of(index * width, width), width)

    own = (
        pltpu.make_async_copy(keys.at[:, lanes(z, HEAD_DIM)], kv.at[z, 0, core, y, place], local_sem.at[0]),
        pltpu.make_async_copy(values.at[:, lanes(z, HEAD_DIM)], kv.at[z, 1, core, y, place], local_sem.at[1]),
        pltpu.make_async_copy(queries.at[:, lanes(z, WIDE)], qbuf.at[z], local_sem.at[2]),
    )
    for copy in own:
        copy.start()

    barrier = pltpu.get_barrier_semaphore()
    greeted = [along_z(step)[1] for step in NEAR_FIRST]
    greeted += [along(step) for along in (along_x, along_y) for step in (1, 2, 3)] + [twin]
    for device in greeted:
        pl.semaphore_signal(barrier, inc=1, device_id=device, device_id_type=MESH)
    pl.semaphore_wait(barrier, len(greeted))

    def remote(src, dst, send, recv, device):
        return pltpu.make_async_remote_copy(
            src_ref=src, dst_ref=dst, send_sem=send, recv_sem=recv, device_id=device, device_id_type=MESH
        )

    def kv_copy(step, which):
        other, device = along_z(step)
        return remote(
            (keys, values)[which].at[:, lanes(other, HEAD_DIM)], kv.at[z, which, core, y, place],
            kv_send.at[which, step], kv_recv.at[which, step], device,
        )

    def q_copy(step):
        other, device = along_z(step)
        return remote(queries.at[:, lanes(other, WIDE)], qbuf.at[z], q_send.at[step], q_recv.at[step], device)

    for step in NEAR_FIRST:
        for which in range(2):
            kv_copy(step, which).start()
    for step in NEAR_FIRST:
        q_copy(step).start()

    def planes(phase):
        start, stop = PHASES[phase]
        return pl.ds(start, stop - start)

    def one_copy(part, which, step):
        some = planes(0) if part == 0 else pl.ds(PHASES[1][0], PLANES - PHASES[1][0])
        ref = kv.at[some, which, core, y, place]
        device = (along_x, along_y)[which](step)
        return remote(ref, ref, one_send.at[part, which, step], one_recv.at[part, which, step], device)

    def two_copy(phase, which, step):
        ref = (kv.at[planes(phase), 0, core, y], kv.at[planes(phase), 1, core, :, place])[which]
        device = (along_y, along_x)[which](step)
        return remote(ref, ref, two_send.at[phase, which, step], two_recv.at[phase, which, step], device)

    def twin_copy(phase):
        ref = kv.at[planes(phase), :, core]
        return remote(ref, ref, twin_send.at[phase], twin_recv.at[phase], twin)

    six = [(which, step) for step in (1, 3, 2) for which in range(2)]

    def spread(phase):
        if phase < 2:
            for which, step in six:
                one_copy(phase, which, step).wait_recv()
        for which, step in six:
            two_copy(phase, which, step).start()

    def pair(phase):
        for which, step in six:
            two_copy(phase, which, step).wait_recv()
        twin_copy(phase).start()

    def slice_of(plane):
        block = qbuf[plane]
        return jnp.concatenate([block[:, h * HEAD_DIM : (h + 1) * HEAD_DIM] for h in range(GROUP)], axis=0)

    def visible(plane, key_plane):
        row = lax.broadcasted_iota(jnp.int32, (ROWS, KEYS), 0)
        index = lax.broadcasted_iota(jnp.int32, (ROWS, KEYS), 1)
        query = (y * SIDE + place) * (2 * BLOCK) + core * BLOCK + row % BLOCK
        key = (index // BLOCK) % (SIDE * SIDE) * (2 * BLOCK) + index // (KEYS // 2) * BLOCK + index % BLOCK
        return query + (plane - key_plane) * KEYS >= key

    scores = (score_a, score_b)

    def multiply(item, n):
        plane, key_plane, _ = item
        scores[n % 2][...] = lax.dot_general(
            slice_of(plane), kv[key_plane, 0].reshape(KEYS, HEAD_DIM), TRANSPOSED,
            preferred_element_type=jnp.float32,
        )

    def soften(item, n):
        plane, key_plane, masked = item
        first = key_plane == 0
        score = scores[n % 2][...]
        if masked:
            score = jnp.where(visible(plane, key_plane), score, LOW)
        top = jnp.broadcast_to(jnp.max(score, axis=1, keepdims=True), (ROWS, HEAD_DIM))
        if not first:
            before = tops[plane]
            top = jnp.maximum(before, top)
            rescale = jnp.exp2((before - top) * SCALE)
        weight = jnp.exp2((score - jnp.tile(top, (1, KEYS // HEAD_DIM))) * SCALE)
        tops[plane] = top
        mixed = jnp.dot(
            weight.astype(jnp.bfloat16), kv[key_plane, 1].reshape(KEYS, HEAD_DIM),
            preferred_element_type=jnp.float32,
        )
        partial = weight[:, :HEAD_DIM]
        for column in range(1, KEYS // HEAD_DIM):
            partial = partial + weight[:, column * HEAD_DIM : (column + 1) * HEAD_DIM]
        if first:
            acc[plane], sums[plane] = mixed, partial
        else:
            acc[plane], sums[plane] = acc[plane] * rescale + mixed, sums[plane] * rescale + partial

    def sweep(items):
        multiply(items[0], 0)
        for n, item in enumerate(items):
            if n + 1 < len(items):
                multiply(items[n + 1], n + 1)
            soften(item, n)
            if isinstance(item[0], int) and item[0] == item[1]:
                finish(item[0])

    def o_copy(plane):
        return remote(
            obuf.at[plane], out.at[:, lanes(z, WIDE)], o_send.at[plane], o_recv.at[z], at(x, y, plane, core)
        )

    own_out = pltpu.make_async_copy(obuf.at[z], out.at[:, lanes(z, WIDE)], local_sem.at[3])

    def finish(plane):
        total = jnp.sum(sums[plane], axis=1, keepdims=True)
        result = (acc[plane] / total).astype(jnp.bfloat16)
        for h in range(GROUP):
            obuf[plane, :, h * HEAD_DIM : (h + 1) * HEAD_DIM] = result[h * BLOCK : (h + 1) * BLOCK]
        pl.when(plane != z)(lambda: o_copy(plane).start())
        pl.when(plane == z)(lambda: own_out.start())

    for copy in own[:2]:
        copy.wait()
    for step in NEAR_FIRST:
        for which in range(2):
            kv_copy(step, which).wait_recv()
    for part in range(2):
        for which, step in six:
            one_copy(part, which, step).start()
    def follow(phase):
        for which, step in six:
            two_copy(phase - 1, which, step).wait_send()
        spread(phase)

    def steps(*near):
        return [((z + step) % PLANES, 0, True) for step in near]

    def pairs(plane, start, stop):
        return [(plane, key_plane, plane == key_plane) for key_plane in range(start, stop)]

    spread(0)
    follow(1)
    pair(0)
    follow(2)
    own[2].wait()
    for step in (1, 7, 2, 6):
        q_copy(step).wait_recv()
    twin_copy(0).wait_recv()
    sweep(steps(0, 1, 7, 2, 6))
    pair(1)
    follow(3)
    for step in (3, 5, 4):
        q_copy(step).wait_recv()
    sweep(steps(3, 5, 4))
    finish(0)
    twin_copy(1).wait_recv()
    sweep(pairs(1, 1, 2) + pairs(2, 1, 3) + pairs(3, 1, 3))
    pair(2)
    follow(4)
    sweep(pairs(4, 1, 3) + pairs(5, 1, 3))
    twin_copy(2).wait_recv()
    sweep(pairs(3, 3, 4) + pairs(4, 3, 5) + pairs(5, 3, 4))
    pair(3)
    sweep(pairs(5, 4, 5) + pairs(6, 1, 3))
    twin_copy(3).wait_recv()
    sweep(pairs(5, 5, 6) + pairs(6, 3, 7))
    pair(4)
    sweep(pairs(7, 1, 7))
    twin_copy(4).wait_recv()
    sweep(pairs(7, 7, 8))

    for which, step in six:
        two_copy(4, which, step).wait_send()
    for step in NEAR_FIRST:
        for which in range(2):
            kv_copy(step, which).wait_send()
        q_copy(step).wait_send()
    for part in range(2):
        for which, step in six:
            one_copy(part, which, step).wait_send()
    for phase in range(len(PHASES)):
        twin_copy(phase).wait_send()
    own_out.wait()
    for plane in range(PLANES):

        @pl.when(plane != z)
        def _():
            o_copy(plane).wait_send()
            ref = out.at[:, lanes(plane, WIDE)]
            remote(ref, ref, o_send.at[plane], o_recv.at[plane], at(x, y, plane, core)).wait_recv()


def on_device(queries, keys, values):
    anywhere = pl.BlockSpec(memory_space=pl.ANY)
    return pl.pallas_call(
        kernel,
        out_shape=jax.ShapeDtypeStruct(queries.shape, jnp.bfloat16),
        in_specs=[anywhere] * 3,
        out_specs=anywhere,
        scratch_shapes=[
            pltpu.VMEM((PLANES, BLOCK, WIDE), jnp.bfloat16),
            pltpu.VMEM((PLANES, 2, 2, SIDE, SIDE, BLOCK, HEAD_DIM), jnp.bfloat16),
            pltpu.VMEM((PLANES, BLOCK, WIDE), jnp.bfloat16),
            pltpu.VMEM((PLANES, ROWS, HEAD_DIM), jnp.float32),
            pltpu.VMEM((PLANES, ROWS, HEAD_DIM), jnp.float32),
            pltpu.VMEM((PLANES, ROWS, HEAD_DIM), jnp.float32),
            pltpu.VMEM((ROWS, KEYS), jnp.float32),
            pltpu.VMEM((ROWS, KEYS), jnp.float32),
            pltpu.SemaphoreType.DMA((4,)),
            pltpu.SemaphoreType.DMA((PLANES,)),
            pltpu.SemaphoreType.DMA((PLANES,)),
            pltpu.SemaphoreType.DMA((2, PLANES)),
            pltpu.SemaphoreType.DMA((2, PLANES)),
            pltpu.SemaphoreType.DMA((2, 2, SIDE)),
            pltpu.SemaphoreType.DMA((2, 2, SIDE)),
            pltpu.SemaphoreType.DMA((len(PHASES), 2, SIDE)),
            pltpu.SemaphoreType.DMA((len(PHASES), 2, SIDE)),
            pltpu.SemaphoreType.DMA((len(PHASES),)),
            pltpu.SemaphoreType.DMA((len(PHASES),)),
            pltpu.SemaphoreType.DMA((PLANES,)),
            pltpu.SemaphoreType.DMA((PLANES,)),
        ],
        compiler_params=pltpu.CompilerParams(
            collective_id=0, has_side_effects=True, vmem_limit_bytes=60 * 2**20
        ),
    )(queries, keys, values)


def solution(mesh):
    spec = P(("seq", "head"), None)
    return jax.shard_map(on_device, mesh=mesh, in_specs=(spec,) * 3, out_specs=spec, check_vma=False)
```
